512 devices in a mesh: replica: 64 (over x, y, core), tensor: 8 (over z).
Axes of the slice: x: 4, y: 8, z: 8, core: 2. Of those that a mesh axis runs over, the one named last changes fastest.
Arguments:
- hidden: bfloat16 [65536, 8192], P('replica', 'tensor'), may hold values from -250 to 250
- norm_gain: bfloat16 [8192], P('tensor'), may hold values from 0.099609375 to 1.8984375
- layer_weight: bfloat16 [64, 8192, 1024], P('replica', 'tensor'), may hold values from -0.0625 to 0.0625
- layer_bias: bfloat16 [64, 1024], P('replica', 'tensor'), may hold values from -3 to 3
- lengths: int32 [64], replicated, may hold values from 1 to 1024, 32768 in all
Outputs:
- keys: bfloat16 [65536, 1024], P('replica', 'tensor')
The draws below stay inside these ranges and needn't reach their ends.
Inputs may be any that keep to these rules, and one draw needn't show every extreme that they name: Replica r's prompt fills the first lengths[r] rows of its block; some replica's prompt fills its whole block.
All inputs are finite; a program needn't handle non-finite values.
Results may differ from the reference program's by a relative error of at most 0.0046.
Values may be sent and summed in bfloat16 or wider, within the bound.
A program may use at most 64 MiB of HBM per device.

```python
import math
import jax
import jax.numpy as jnp
import numpy as np
from jax import lax

D = 8192
HEAD = 128
GROUP = 4
TOK_DEV = 1024
KVD = 1024
TOKENS = 65536
N_REPLICA = 64


def draw_hidden(key, part):
    key = jax.random.fold_in(key, 7)
    key_core, key_rows, key_cols = jax.random.split(key, 3)
    row_scale = 10.0 ** jax.random.uniform(key_rows, (TOKENS, 1), jnp.float32)
    column_scale = 10.0 ** jax.random.uniform(key_cols, (1, D), jnp.float32)
    ramp_scale = jnp.sqrt(1.0 + 2.0 * jnp.arange(D, dtype=jnp.float32) / D)[None, :]
    core_part = jnp.clip(jax.random.normal(key_core, (TOKENS, D), jnp.float32), -4.0, 4.0)
    values = 0.3 * core_part * row_scale * column_scale * ramp_scale
    return values.astype(jnp.bfloat16)


def level_of(rng, shape, pieces, least, largest):
    level, own = 1.0, jax.random.fold_in(rng, 6)
    for axis_at, shards_of in pieces:
        draws = jnp.exp(jax.random.uniform(jax.random.fold_in(own, axis_at), (shards_of,), jnp.float32, least / len(pieces), largest / len(pieces)))
        level = level * jnp.repeat(draws, shape[axis_at] // shards_of).reshape([-1 if axis == axis_at else 1 for axis in range(len(shape))])
    return level


def profile(count, total, reach, lean):
    loads = [(1 << 20) // math.isqrt(grade ** lean) + 1 for grade in range(2, count + 1)]
    surplus, counts = total - reach - (count - 1), [1] * (count - 1)
    while surplus > 0:
        movable = [i for i in range(count - 1) if counts[i] < reach]
        whole, remaining = sum([loads[i] for i in movable]), surplus
        for i in movable:
            extra = min(reach - counts[i], max(1, remaining * loads[i] // whole), surplus)
            counts[i] = counts[i] + extra
            surplus = surplus - extra
    return np.array([reach] + counts)


def ragged(stream_key, number_of, total, most, skew):
    if number_of == 2:
        one = jax.random.randint(stream_key, (), max(1, total - most), min(most, total - 1) + 1)
        return jnp.stack([one, total - one])
    sizes = jnp.asarray(profile(number_of, total, most, skew), jnp.int32)
    twos = (number_of - 1) // 2
    source_of, taker = sizes[1:1 + 2 * twos:2], sizes[2:2 + 2 * twos:2]
    slack = jnp.minimum(source_of - 1, most - taker)
    passed = jax.random.randint(jax.random.fold_in(stream_key, 1), (twos,), 0, 1 << 20) % (slack + 1)
    sizes = sizes.at[1:1 + 2 * twos:2].set(source_of - passed).at[2:2 + 2 * twos:2].set(taker + passed)
    return sizes[jax.random.permutation(jax.random.fold_in(stream_key, 2), number_of)]


def bell_draw(key, dims, width, most, cuts=(), kind=jnp.bfloat16):
    values = width * jax.random.normal(key, dims, jnp.float32)
    if cuts:
        values = values * level_of(key, dims, cuts, -0.22, 0.18)
    return jnp.clip(values, -most, most).astype(kind)


def setup_inputs(seed: int = 0) -> dict:
    arg_keys = jax.random.split(jax.random.key(seed), 6)
    hidden = draw_hidden(jax.random.fold_in(arg_keys[5], 71), 0)
    norm_gain = jnp.clip(1.0 + 0.18 * jax.random.normal(arg_keys[1], (D,), jnp.float32), 0.099609375, 1.8984375).astype(jnp.bfloat16)
    layer_weight = bell_draw(arg_keys[2], (N_REPLICA, D, KVD), D ** -0.5, 0.0625, ((0, 64), (1, 8)))
    layer_bias = bell_draw(arg_keys[3], (N_REPLICA, KVD), 0.5, 3.0, ((0, 64), (1, 8)))
    lengths = ragged(arg_keys[4], N_REPLICA, N_REPLICA * TOK_DEV // 2, TOK_DEV, 2).astype(jnp.int32)
    return {"hidden": hidden, "norm_gain": norm_gain, "layer_weight": layer_weight, "layer_bias": layer_bias, "lengths": lengths}


epsilon = 1e-06
rope_base = 1000000.0

def rotate(projected, positions):
    row_count = projected.shape[0]
    per_head = projected.reshape(row_count, -1, HEAD)
    half_size = HEAD // 2
    frequency = 1.0 / rope_base ** (jnp.arange(half_size, dtype=jnp.float32) * (2.0 / HEAD))
    angles = positions[:, None] * frequency[None, :]
    cosine = jnp.cos(angles)[:, None, :]
    sine_part = jnp.sin(angles)[:, None, :]
    first_half = per_head[..., :half_size]
    second = per_head[..., half_size:]
    rotated = jnp.concatenate([first_half * cosine - second * sine_part, second * cosine + first_half * sine_part], axis=-1)
    return rotated.reshape(row_count, -1)

def reference(hidden, norm_gain, layer_weight, layer_bias, lengths):
    groups = N_REPLICA // GROUP
    block_rows = GROUP * TOK_DEV
    blocks = hidden.reshape(groups, block_rows, D)
    weights = layer_weight.reshape(groups, GROUP, D, KVD)[:, 0]
    biases = layer_bias.reshape(groups, GROUP, KVD)[:, 0]
    limits = jnp.repeat(lengths.reshape(groups, GROUP), TOK_DEV, axis=1)
    positions = jnp.arange(block_rows, dtype=jnp.int32) % TOK_DEV
    gain_row = norm_gain.astype(jnp.float32)

    def one_group(members):
        row_block, weight, bias_row, row_limit = members
        values = row_block.astype(jnp.float32)
        mean_square = lax.optimization_barrier(jnp.mean(values * values, axis=1))
        normed = (values * lax.rsqrt(mean_square + epsilon)[:, None] * gain_row[None, :]).astype(jnp.bfloat16)
        projected = jnp.dot(normed, weight, preferred_element_type=jnp.float32) + bias_row.astype(jnp.float32)[None, :]
        rotated = rotate(projected, positions.astype(jnp.float32))
        return jnp.where((positions < row_limit)[:, None], rotated, jnp.float32(0.0)).astype(jnp.bfloat16)
    result = lax.map(one_group, (blocks, weights, biases, limits))
    return result.reshape(N_REPLICA * TOK_DEV, KVD)
```

```python
import functools

import jax
import jax.numpy as jnp
import numpy as np
from jax import lax
from jax.experimental import pallas as pl
from jax.experimental.pallas import tpu as pltpu
from jax.sharding import PartitionSpec as P

HEAD = 128
GROUP = 4
SUB = 256
EPSILON = 1e-06
ROPE_BASE = 1000000.0
MESH = pl.DeviceIdType.MESH


def rope_table(rows):
    half = HEAD // 2
    exponent = np.arange(half, dtype=np.float32) * np.float32(2.0 / HEAD)
    frequency = np.float32(1.0) / np.power(np.float32(ROPE_BASE), exponent)
    angles = np.arange(rows, dtype=np.float32)[:, None] * frequency[None, :]
    angles = angles.astype(np.float64)
    return np.concatenate([np.cos(angles), np.sin(angles)], axis=1).astype(np.float32)


def kernel(
    ring,
    hid, gain, weight, bias, lens, table,
    out,
    h_v, n_v, w_v, t_v, squares, bias_v, send_v, recv_v,
    h_sem, t_sem, w_sem, head_send, half_recv, swap_send, swap_recv,
    square_send, square_recv, bias_send, bias_recv, ring_send, ring_recv,
):
    rows, depth = h_v.shape
    subs = rows // SUB
    half_rows = depth // 2
    replica = lax.axis_index("replica")
    z = lax.axis_index("tensor")
    slot = lax.rem(replica, GROUP)
    head = replica - slot
    partner = head + 2 + (1 - lax.rem(slot, 2))

    def at(distance):
        return lax.rem(z + (distance + ring), ring)

    order = [ring // 2]
    for distance in range(ring // 2 - 1, 0, -1):
        order += [distance, -distance]
    order += [0]

    def columns(distance):
        return pl.ds(pl.multiple_of(at(distance) * HEAD, HEAD), HEAD)

    barrier = pltpu.get_barrier_semaphore()
    for distance in range(1, ring):
        pl.semaphore_signal(barrier, inc=1, device_id={"tensor": at(distance)}, device_id_type=MESH)
    for step in range(1, GROUP):
        other = head + lax.rem(slot + step, GROUP)
        pl.semaphore_signal(barrier, inc=1, device_id={"replica": other}, device_id_type=MESH)

    def load_hidden(block):
        part = pl.ds(block * SUB, SUB)
        return pltpu.make_async_copy(hid.at[part], h_v.at[part], h_sem.at[block])

    def load_weight(i):
        return pltpu.make_async_copy(weight.at[0, :, columns(order[i])], w_v.at[i], w_sem.at[i])

    load_table = pltpu.make_async_copy(table, t_v, t_sem)

    @pl.when(slot == 0)
    def _():
        for i in range(ring):
            load_weight(i).start()

    for block in range(subs):
        load_hidden(block).start()
    load_table.start()

    pl.semaphore_wait(barrier, ring - 1 + GROUP - 1)

    low, high = pl.ds(0, half_rows), pl.ds(half_rows, half_rows)

    def head_copies(i):
        whole = pltpu.make_async_remote_copy(
            src_ref=w_v.at[i], dst_ref=w_v.at[i],
            send_sem=head_send.at[i, 0], recv_sem=w_sem.at[i],
            device_id={"replica": head + 1}, device_id_type=MESH)
        halves = [
            pltpu.make_async_remote_copy(
                src_ref=w_v.at[i, part], dst_ref=w_v.at[i, part],
                send_sem=head_send.at[i, 1 + core], recv_sem=half_recv.at[i],
                device_id={"replica": head + 2 + core}, device_id_type=MESH)
            for core, part in enumerate((low, high))
        ]
        return halves + [whole]

    def bias_copies():
        return [
            pltpu.make_async_remote_copy(
                src_ref=bias_v, dst_ref=bias_v,
                send_sem=bias_send.at[step], recv_sem=bias_recv,
                device_id={"replica": head + step}, device_id_type=MESH)
            for step in range(1, GROUP)
        ]

    @pl.when(slot == 0)
    def _():
        for i in range(ring):
            load_weight(i).wait()
            for copy in head_copies(i):
                copy.start()
        bias_v[...] = jnp.broadcast_to(bias[...], bias_v.shape)
        for copy in bias_copies():
            copy.start()

    for block in range(subs):
        load_hidden(block).wait()
        for i in range(block * SUB // HEAD, (block + 1) * SUB // HEAD):
            values = h_v[pl.ds(i * HEAD, HEAD), :].astype(jnp.float32)
            total = jnp.zeros((HEAD, HEAD), jnp.float32)
            for j in range(depth // HEAD):
                piece = values[:, j * HEAD:(j + 1) * HEAD]
                total = total + piece * piece
            squares[0, pl.ds(i, 1), :] = jnp.sum(total.T, axis=0, keepdims=True)

    def square_copy(distance):
        return pltpu.make_async_remote_copy(
            src_ref=squares.at[0], dst_ref=squares.at[distance],
            send_sem=square_send.at[distance], recv_sem=square_recv.at[distance],
            device_id={"tensor": at(distance)}, device_id_type=MESH)

    for distance in range(1, ring):
        square_copy(distance).start()
    for distance in range(1, ring):
        square_copy(distance).wait_recv()

    sums = squares[0]
    for distance in range(1, ring):
        sums = sums + squares[distance]
    inverse = lax.rsqrt(sums / (depth * ring) + EPSILON)
    gain_row = gain[...].astype(jnp.float32)
    for i in range(rows // HEAD):
        part = pl.ds(i * HEAD, HEAD)
        scale = jnp.broadcast_to(inverse[i:i + 1, :], (HEAD, HEAD)).T
        for j in range(depth // HEAD):
            cols = pl.ds(j * HEAD, HEAD)
            values = h_v[part, cols].astype(jnp.float32)
            n_v[part, cols] = (values * scale * gain_row[:, j * HEAD:(j + 1) * HEAD]).astype(jnp.bfloat16)

    def swap_copy(i, part, to):
        return pltpu.make_async_remote_copy(
            src_ref=w_v.at[i, part], dst_ref=w_v.at[i, part],
            send_sem=swap_send.at[i], recv_sem=swap_recv.at[i],
            device_id={"replica": to}, device_id_type=MESH)

    def take_weight(i):
        @pl.when(slot == 1)
        def _():
            pltpu.make_async_remote_copy(
                src_ref=w_v.at[i], dst_ref=w_v.at[i],
                send_sem=head_send.at[i, 0], recv_sem=w_sem.at[i],
                device_id={"replica": head + 1}, device_id_type=MESH).wait_recv()

        for core, (mine, theirs) in enumerate(((low, high), (high, low))):
            @pl.when(slot == 2 + core)
            def _():
                pltpu.make_async_remote_copy(
                    src_ref=w_v.at[i, mine], dst_ref=w_v.at[i, mine],
                    send_sem=head_send.at[i, 1 + core], recv_sem=half_recv.at[i],
                    device_id={"replica": head}, device_id_type=MESH).wait_recv()
                swap_copy(i, mine, partner).start()
                swap_copy(i, theirs, partner).wait_recv()

    def product(i, sub):
        return jnp.dot(n_v[pl.ds(sub * SUB, SUB), :], w_v[i], preferred_element_type=jnp.float32)

    def hop(distance, positive):
        return (abs(distance) - 1) + (0 if positive else ring // 2)

    def ring_copy(distance, positive, sub):
        h = hop(distance, positive)
        part = pl.ds(sub * SUB, SUB)
        return pltpu.make_async_remote_copy(
            src_ref=send_v.at[h, part], dst_ref=recv_v.at[h, part],
            send_sem=ring_send.at[h, sub], recv_sem=ring_recv.at[h, sub],
            device_id={"tensor": at(1 if positive else -1)}, device_id_type=MESH)

    def incoming(distance, positive, sub):
        ring_copy(distance, positive, sub).wait_recv()
        return recv_v[hop(distance, positive), pl.ds(sub * SUB, SUB)].astype(jnp.float32)

    started = []
    plus_first = [s for s in range(subs) if s < subs // 2]
    minus_first = [s for s in range(subs) if s >= subs // 2]
    for i, distance in enumerate(order[:-1]):
        take_weight(i)
        if distance == ring // 2:
            work = [(True, s) for s in plus_first] + [(False, s) for s in minus_first]
        elif distance > 0:
            work = [(True, s) for s in minus_first + plus_first]
        else:
            work = [(False, s) for s in plus_first + minus_first]
        for positive, sub in work:
            value = product(i, sub)
            step = abs(distance)
            far = step + 1
            first = plus_first if positive else minus_first
            if far < ring // 2 or (far == ring // 2 and sub in first):
                value = value + incoming(far, positive, sub)
            send_v[hop(step, positive), pl.ds(sub * SUB, SUB)] = value.astype(jnp.bfloat16)
            copy = ring_copy(step, positive, sub)
            copy.start()
            started.append(copy)

    last = len(order) - 1
    take_weight(last)
    load_table.wait()

    @pl.when(slot > 0)
    def _():
        pltpu.make_async_remote_copy(
            src_ref=bias_v, dst_ref=bias_v,
            send_sem=bias_send.at[1], recv_sem=bias_recv,
            device_id={"replica": head}, device_id_type=MESH).wait_recv()

    bias_row = bias_v[0:1, :].astype(jnp.float32)
    own_length = lens[replica]
    lane = lax.broadcasted_iota(jnp.int32, (SUB, HEAD), 1)
    row = lax.broadcasted_iota(jnp.int32, (SUB, HEAD), 0)
    in_first = lane < HEAD // 2
    for sub in minus_first + plus_first:
        part = pl.ds(sub * SUB, SUB)
        value = product(last, sub)
        value = value + incoming(1, True, sub)
        value = value + incoming(1, False, sub)
        value = value + bias_row
        trig = t_v[part, :]
        swapped = pltpu.roll(trig, HEAD // 2, 1)
        cosine = jnp.where(in_first, trig, swapped)
        sine = jnp.where(in_first, -swapped, trig)
        rotated = value * cosine + pltpu.roll(value, HEAD // 2, 1) * sine
        kept = jnp.where(row + sub * SUB < own_length, rotated, 0.0)
        out[part, :] = kept.astype(jnp.bfloat16)

    for copy in started:
        copy.wait_send()
    for distance in range(1, ring):
        square_copy(distance).wait_send()

    @pl.when(slot == 0)
    def _():
        for i in range(ring):
            for copy in head_copies(i):
                copy.wait_send()
        for copy in bias_copies():
            copy.wait_send()

    for core, mine in enumerate((low, high)):
        @pl.when(slot == 2 + core)
        def _():
            for i in range(ring):
                swap_copy(i, mine, partner).wait_send()


def solution(mesh):
    ring = mesh.shape["tensor"]

    def local(hidden, norm_gain, layer_weight, layer_bias, lengths):
        rows, depth = hidden.shape
        subs = rows // SUB
        table = jnp.asarray(rope_table(rows))
        vmem = pl.BlockSpec(memory_space=pltpu.VMEM)
        hbm = pl.BlockSpec(memory_space=pl.ANY)
        dma = pltpu.SemaphoreType.DMA
        return pl.pallas_call(
            functools.partial(kernel, ring),
            out_shape=jax.ShapeDtypeStruct((rows, HEAD), jnp.bfloat16),
            in_specs=[hbm, vmem, hbm, vmem, pl.BlockSpec(memory_space=pltpu.SMEM), hbm],
            out_specs=vmem,
            scratch_shapes=[
                pltpu.VMEM((rows, depth), jnp.bfloat16),
                pltpu.VMEM((rows, depth), jnp.bfloat16),
                pltpu.VMEM((ring, depth, HEAD), jnp.bfloat16),
                pltpu.VMEM((rows, HEAD), jnp.float32),
                pltpu.VMEM((ring, rows // HEAD, HEAD), jnp.float32),
                pltpu.VMEM((16, HEAD), jnp.bfloat16),
                pltpu.VMEM((ring, rows, HEAD), jnp.bfloat16),
                pltpu.VMEM((ring, rows, HEAD), jnp.bfloat16),
                dma((subs,)),
                dma,
                dma((ring,)),
                dma((ring, 3)),
                dma((ring,)),
                dma((ring,)),
                dma((ring,)),
                dma((ring,)),
                dma((ring,)),
                dma((GROUP,)),
                dma,
                dma((ring, subs)),
                dma((ring, subs)),
            ],
            compiler_params=pltpu.CompilerParams(
                collective_id=0, has_side_effects=True, vmem_limit_bytes=48 * 1024 * 1024
            ),
            name="keys",
        )(hidden, norm_gain.reshape(1, depth), layer_weight, layer_bias, lengths, table)

    in_specs = (
        P("replica", "tensor"),
        P("tensor"),
        P("replica", "tensor", None),
        P("replica", "tensor"),
        P(),
    )
    return jax.shard_map(
        local, mesh=mesh, in_specs=in_specs, out_specs=P("replica", "tensor"), check_vma=False
    )
```

```python
import functools

import jax
import jax.numpy as jnp
import numpy as np
from jax import lax
from jax.experimental import pallas as pl
from jax.experimental.pallas import tpu as pltpu
from jax.sharding import PartitionSpec as P

HEAD = 128
HALF = HEAD // 2
GROUP = 4
SUB = 512
EPSILON = 1e-06
ROPE_BASE = 1000000.0
MESH = pl.DeviceIdType.MESH


def rope_table(rows):
    exponent = np.arange(HALF, dtype=np.float32) * np.float32(2.0 / HEAD)
    frequency = np.float32(1.0) / np.power(np.float32(ROPE_BASE), exponent)
    angles = np.arange(rows, dtype=np.float32)[:, None] * frequency[None, :]
    angles = angles.astype(np.float64)
    return np.concatenate([np.cos(angles), np.sin(angles)], axis=1).astype(np.float32)


def trade(x, y):
    first = lax.broadcasted_iota(jnp.int32, x.shape, 1) < HALF
    x_other, y_other = pltpu.roll(x, HALF, 1), pltpu.roll(y, HALF, 1)
    return jnp.where(first, x, y_other), jnp.where(first, x_other, y)


def kernel(
    ring,
    hid, gain_h, weight, bias_h, lens_h, table,
    out,
    h_v, n_v, w_n, w_v, t_v, gain, bias, lens, squares, bias_v, send_v, recv_v,
    h_sem, t_sem, small_sem, n_sem, w_sem, head_send, pass_send,
    square_send, square_recv, bias_send, bias_recv, ring_send, ring_recv,
):
    rows, depth = h_v.shape
    subs = rows // SUB
    far = ring // 2
    replica = lax.axis_index("replica")
    z = lax.axis_index("tensor")
    slot = lax.rem(replica, GROUP)
    head = replica - slot

    def at(distance):
        return lax.rem(z + (distance + ring), ring)

    def columns(distance):
        return pl.ds(pl.multiple_of(at(distance) * HEAD, HEAD), HEAD)

    barrier = pltpu.get_barrier_semaphore()
    for step in range(1, GROUP):
        other = head + lax.rem(slot + step, GROUP)
        pl.semaphore_signal(barrier, inc=1, device_id={"replica": other}, device_id_type=MESH)
    for distance in range(1, ring):
        pl.semaphore_signal(barrier, inc=1, device_id={"tensor": at(distance)}, device_id_type=MESH)
    waits = ring - 1 + GROUP - 1

    def load_hidden(block):
        part = pl.ds(block * SUB, SUB)
        return pltpu.make_async_copy(hid.at[part], h_v.at[part], h_sem.at[block])

    last = ring - 1

    def load_whole(i):
        distance = far if i == 0 else 0
        return pltpu.make_async_copy(weight.at[0, :, columns(distance)], w_v.at[i], w_sem.at[i])

    def load_part(k, sign):
        j = 2 * (k - 1) + (0 if sign > 0 else 1)
        return pltpu.make_async_copy(weight.at[0, :, columns(sign * k)], w_n.at[j], n_sem.at[j])

    load_table = pltpu.make_async_copy(table, t_v, t_sem)
    load_gain = pltpu.make_async_copy(gain_h, gain, small_sem.at[0])
    load_bias = pltpu.make_async_copy(bias_h, bias, small_sem.at[1])
    load_lens = pltpu.make_async_copy(lens_h, lens, small_sem.at[2])

    @pl.when(slot == 0)
    def _():
        load_whole(0).start()
        for k in range(far - 1, 0, -1):
            load_part(k, 1).start()
            load_part(k, -1).start()
        load_whole(last).start()

    load_gain.start()
    for block in range(subs):
        load_hidden(block).start()
    load_bias.start()
    load_lens.start()
    load_table.start()

    def block_of(k, half):
        return 1 + 2 * (far - 1 - k) + half

    def mix(k):
        load_part(k, 1).wait()
        load_part(k, -1).wait()
        j = 2 * (k - 1)
        for r in range(0, depth, HEAD):
            part = pl.ds(r, HEAD)
            plus = w_n[j, part].astype(jnp.float32)
            minus = w_n[j + 1, part].astype(jnp.float32)
            for half, mixed in enumerate(trade(plus, minus)):
                w_v[block_of(k, half), part] = mixed.astype(jnp.bfloat16)

    def head_copies(i):
        return [
            pltpu.make_async_remote_copy(
                src_ref=w_v.at[i], dst_ref=w_v.at[i],
                send_sem=head_send.at[i, to - 1], recv_sem=w_sem.at[i],
                device_id={"replica": head + to}, device_id_type=MESH)
            for to in (2, 1)
        ]

    def pass_copy(i):
        return pltpu.make_async_remote_copy(
            src_ref=w_v.at[i], dst_ref=w_v.at[i],
            send_sem=pass_send.at[i], recv_sem=w_sem.at[i],
            device_id={"replica": head + 3}, device_id_type=MESH)

    def bias_copies():
        return [
            pltpu.make_async_remote_copy(
                src_ref=bias_v, dst_ref=bias_v,
                send_sem=bias_send.at[step], recv_sem=bias_recv,
                device_id={"replica": head + step}, device_id_type=MESH)
            for step in range(1, GROUP)
        ]

    def prepare():
        load_gain.wait()
        gain_row = gain[...].astype(jnp.float32).reshape(1, depth)
        for block in range(subs):
            load_hidden(block).wait()
            for i in range(block * SUB // HEAD, (block + 1) * SUB // HEAD):
                part = pl.ds(i * HEAD, HEAD)
                total = jnp.zeros((HEAD, HEAD), jnp.float32)
                for j in range(depth // HEAD):
                    cols = slice(j * HEAD, (j + 1) * HEAD)
                    piece = h_v[part, cols].astype(jnp.float32)
                    total = total + piece * piece
                    n_v[part, cols] = (piece * gain_row[:, cols]).astype(jnp.bfloat16)
                squares[0, pl.ds(i, 1), :] = jnp.sum(total.T, axis=0, keepdims=True)

    @pl.when(slot == 0)
    def _():
        load_whole(0).wait()
        mix(far - 1)
        pl.semaphore_wait(barrier, waits)
        for i in range(ring):
            if i > 2 and i < last and i % 2 == 1:
                mix(far - 1 - i // 2)
            if i == last:
                load_whole(last).wait()
            for copy in head_copies(i):
                copy.start()
        prepare()

    @pl.when(slot > 0)
    def _():
        prepare()
        pl.semaphore_wait(barrier, waits)

    def square_copy(distance):
        return pltpu.make_async_remote_copy(
            src_ref=squares.at[0], dst_ref=squares.at[distance],
            send_sem=square_send.at[distance], recv_sem=square_recv.at[distance],
            device_id={"tensor": at(distance)}, device_id_type=MESH)

    for distance in range(1, ring):
        square_copy(distance).start()
    load_bias.wait()

    @pl.when(slot == 0)
    def _():
        bias_v[...] = jnp.broadcast_to(bias[...], bias_v.shape)
        for copy in bias_copies():
            copy.start()

    def take_weight(i):
        @pl.when(slot > 0)
        def _():
            pass_copy(i).wait_recv()

        @pl.when(slot == 2)
        def _():
            pass_copy(i).start()

    def product(i, sub):
        return jnp.dot(n_v[pl.ds(sub * SUB, SUB), :], w_v[i], preferred_element_type=jnp.float32)

    def ring_copy(distance, positive, half, sub):
        h = (distance - 1) + (0 if positive else far)
        part = pl.ds(sub * SUB // 2, SUB // 2)
        return pltpu.make_async_remote_copy(
            src_ref=send_v.at[h, half, part], dst_ref=recv_v.at[h, half, part],
            send_sem=ring_send.at[h, half, sub], recv_sem=ring_recv.at[h, half, sub],
            device_id={"tensor": at(1 if positive else -1)}, device_id_type=MESH)

    def incoming(distance, positive, half, sub):
        ring_copy(distance, positive, half, sub).wait_recv()
        h = (distance - 1) + (0 if positive else far)
        return recv_v[h, half, pl.ds(sub * SUB // 2, SUB // 2)].astype(jnp.float32)

    started = []

    def forward(distance, positive, half, sub, value):
        h = (distance - 1) + (0 if positive else far)
        send_v[h, half, pl.ds(sub * SUB // 2, SUB // 2)] = value.astype(jnp.bfloat16)
        copy = ring_copy(distance, positive, half, sub)
        copy.start()
        started.append(copy)

    def starts(positive, sub):
        return (sub < subs // 2) == positive

    take_weight(0)
    for sub in range(subs):
        value = product(0, sub)
        for half, packed in enumerate(trade(value[:SUB // 2], value[SUB // 2:])):
            forward(far, starts(True, sub), half, sub, packed)

    for k in range(far - 1, 0, -1):
        for half in (0, 1):
            take_weight(block_of(k, half))
            for sub in range(subs):
                value = product(block_of(k, half), sub)
                plus, minus = trade(value[:SUB // 2], value[SUB // 2:])
                ways = [(True, plus), (False, minus)]
                if k == far - 1 and starts(True, sub):
                    ways = ways[::-1]
                for positive, packed in ways:
                    if k < far - 1 or starts(positive, sub):
                        packed = packed + incoming(k + 1, positive, half, sub)
                    forward(k, positive, half, sub, packed)

    take_weight(last)
    load_table.wait()
    load_lens.wait()
    sums = squares[0]
    for distance in range(1, ring):
        square_copy(distance).wait_recv()
        sums = sums + squares[distance]
    inverse = lax.rsqrt(sums / (depth * ring) + EPSILON)

    @pl.when(slot > 0)
    def _():
        pltpu.make_async_remote_copy(
            src_ref=bias_v, dst_ref=bias_v,
            send_sem=bias_send.at[1], recv_sem=bias_recv,
            device_id={"replica": head}, device_id_type=MESH).wait_recv()

    bias_row = bias_v[0:1, :].astype(jnp.float32)
    own_length = lens[replica]
    lane = lax.broadcasted_iota(jnp.int32, (HEAD, HEAD), 1)
    row = lax.broadcasted_iota(jnp.int32, (HEAD, HEAD), 0)
    in_first = lane < HALF

    def finish(i, value):
        part = pl.ds(i * HEAD, HEAD)
        scale = jnp.broadcast_to(inverse[i:i + 1, :], (HEAD, HEAD)).T
        value = value * scale + bias_row
        trig = t_v[part, :]
        swapped = pltpu.roll(trig, HALF, 1)
        cosine = jnp.where(in_first, trig, swapped)
        sine = jnp.where(in_first, -swapped, trig)
        rotated = value * cosine + pltpu.roll(value, HALF, 1) * sine
        kept = jnp.where(row + i * HEAD < own_length, rotated, 0.0)
        out[part, :] = kept.astype(jnp.bfloat16)

    for sub in range(subs):
        value = product(last, sub)
        halves = [incoming(1, True, half, sub) + incoming(1, False, half, sub) for half in (0, 1)]
        total = value + jnp.concatenate(trade(*halves), axis=0)
        for i in range(SUB // HEAD):
            finish(sub * SUB // HEAD + i, total[i * HEAD:(i + 1) * HEAD])

    for copy in started:
        copy.wait_send()
    for distance in range(1, ring):
        square_copy(distance).wait_send()

    @pl.when(slot == 0)
    def _():
        for i in range(ring):
            for copy in head_copies(i):
                copy.wait_send()
        for copy in bias_copies():
            copy.wait_send()

    @pl.when(slot == 2)
    def _():
        for i in range(ring):
            pass_copy(i).wait_send()


def solution(mesh):
    ring = mesh.shape["tensor"]

    def local(hidden, norm_gain, layer_weight, layer_bias, lengths):
        rows, depth = hidden.shape
        subs = rows // SUB
        far = ring // 2
        table = jnp.asarray(rope_table(rows))
        dma = pltpu.SemaphoreType.DMA
        return pl.pallas_call(
            functools.partial(kernel, ring),
            out_shape=jax.ShapeDtypeStruct((rows, HEAD), jnp.bfloat16),
            in_specs=[pl.BlockSpec(memory_space=pl.ANY)] * 6,
            out_specs=pl.BlockSpec(memory_space=pltpu.VMEM),
            scratch_shapes=[
                pltpu.VMEM((rows, depth), jnp.bfloat16),
                pltpu.VMEM((rows, depth), jnp.bfloat16),
                pltpu.VMEM((ring - 2, depth, HEAD), jnp.bfloat16),
                pltpu.VMEM((ring, depth, HEAD), jnp.bfloat16),
                pltpu.VMEM((rows, HEAD), jnp.float32),
                pltpu.VMEM((depth,), jnp.bfloat16),
                pltpu.VMEM((1, HEAD), jnp.bfloat16),
                pltpu.SMEM(lengths.shape, jnp.int32),
                pltpu.VMEM((ring, rows // HEAD, HEAD), jnp.float32),
                pltpu.VMEM((16, HEAD), jnp.bfloat16),
                pltpu.VMEM((2 * far, 2, rows // 2, HEAD), jnp.bfloat16),
                pltpu.VMEM((2 * far, 2, rows // 2, HEAD), jnp.bfloat16),
                dma((subs,)),
                dma,
                dma((3,)),
                dma((ring - 2,)),
                dma((ring,)),
                dma((ring, 2)),
                dma((ring,)),
                dma((ring,)),
                dma((ring,)),
                dma((GROUP,)),
                dma,
                dma((2 * far, 2, subs)),
                dma((2 * far, 2, subs)),
            ],
            compiler_params=pltpu.CompilerParams(
                collective_id=0, has_side_effects=True, vmem_limit_bytes=60 * 1024 * 1024
            ),
            name="keys",
        )(hidden, norm_gain, layer_weight, layer_bias, lengths, table)

    in_specs = (
        P("replica", "tensor"),
        P("tensor"),
        P("replica", "tensor", None),
        P("replica", "tensor"),
        P(),
    )
    return jax.shard_map(
        local, mesh=mesh, in_specs=in_specs, out_specs=P("replica", "tensor"), check_vma=False
    )
```

```python
import functools

import jax
import jax.numpy as jnp
import numpy as np
from jax import lax
from jax.experimental import pallas as pl
from jax.experimental.pallas import tpu as pltpu
from jax.sharding import PartitionSpec as P

HEAD = 128
HALF = HEAD // 2
GROUP = 4
SUB = 512
MOVED = 128
EPSILON = 1e-06
ROPE_BASE = 1000000.0
MESH = pl.DeviceIdType.MESH


def rope_table(rows):
    exponent = np.arange(HALF, dtype=np.float32) * np.float32(2.0 / HEAD)
    frequency = np.float32(1.0) / np.power(np.float32(ROPE_BASE), exponent)
    angles = np.arange(rows, dtype=np.float32)[:, None] * frequency[None, :]
    angles = angles.astype(np.float64)
    return np.concatenate([np.cos(angles), np.sin(angles)], axis=1).astype(np.float32)


def trade(x, y):
    first = lax.broadcasted_iota(jnp.int32, x.shape, 1) < HALF
    x_other, y_other = pltpu.roll(x, HALF, 1), pltpu.roll(y, HALF, 1)
    return jnp.where(first, x, y_other), jnp.where(first, x_other, y)


def kernel(
    ring,
    hid, gain_h, weight, bias_h, lens_h, table,
    out,
    h_v, n_v, w_n, w_v, t_v, gain, bias, lens, squares, bias_v, sums_v, moved_v, send_v, recv_v,
    h_sem, t_sem, small_sem, n_sem, w_sem, head_send, pass_send,
    square_send, square_recv, bias_send, bias_recv, move_sem, back_sem, ring_send, ring_recv,
):
    rows, depth = h_v.shape
    subs = rows // SUB
    far = ring // 2
    replica = lax.axis_index("replica")
    z = lax.axis_index("tensor")
    slot = lax.rem(replica, GROUP)
    head = replica - slot

    def at(distance):
        return lax.rem(z + (distance + ring), ring)

    def columns(distance):
        return pl.ds(pl.multiple_of(at(distance) * HEAD, HEAD), HEAD)

    barrier = pltpu.get_barrier_semaphore()
    for step in range(1, GROUP):
        other = head + lax.rem(slot + step, GROUP)
        pl.semaphore_signal(barrier, inc=1, device_id={"replica": other}, device_id_type=MESH)
    for distance in range(1, ring):
        pl.semaphore_signal(barrier, inc=1, device_id={"tensor": at(distance)}, device_id_type=MESH)
    waits = ring - 1 + GROUP - 1

    def load_hidden(block):
        part = pl.ds(block * SUB, SUB)
        return pltpu.make_async_copy(hid.at[part], h_v.at[part], h_sem.at[block])

    last = ring - 1

    def load_whole(i):
        distance = far if i == 0 else 0
        return pltpu.make_async_copy(weight.at[0, :, columns(distance)], w_v.at[i], w_sem.at[i])

    def load_part(k, sign):
        j = 2 * (k - 1) + (0 if sign > 0 else 1)
        return pltpu.make_async_copy(weight.at[0, :, columns(sign * k)], w_n.at[j], n_sem.at[j])

    load_table = pltpu.make_async_copy(table, t_v, t_sem)
    load_gain = pltpu.make_async_copy(gain_h, gain, small_sem.at[0])
    load_bias = pltpu.make_async_copy(bias_h, bias, small_sem.at[1])
    load_lens = pltpu.make_async_copy(lens_h, lens, small_sem.at[2])

    @pl.when(slot == 0)
    def _():
        load_whole(0).start()
        for k in range(far - 1, 0, -1):
            load_part(k, 1).start()
            load_part(k, -1).start()
        load_whole(last).start()

    load_gain.start()
    for block in range(subs):
        load_hidden(block).start()
    load_bias.start()
    load_lens.start()
    load_table.start()

    def block_of(k, half):
        return 1 + 2 * (far - 1 - k) + half

    def mix(k):
        load_part(k, 1).wait()
        load_part(k, -1).wait()
        j = 2 * (k - 1)
        for r in range(0, depth, HEAD):
            part = pl.ds(r, HEAD)
            plus = w_n[j, part].astype(jnp.float32)
            minus = w_n[j + 1, part].astype(jnp.float32)
            for half, mixed in enumerate(trade(plus, minus)):
                w_v[block_of(k, half), part] = mixed.astype(jnp.bfloat16)

    def head_copies(i):
        return [
            pltpu.make_async_remote_copy(
                src_ref=w_v.at[i], dst_ref=w_v.at[i],
                send_sem=head_send.at[i, to - 1], recv_sem=w_sem.at[i],
                device_id={"replica": head + to}, device_id_type=MESH)
            for to in (2, 1)
        ]

    def pass_copy(i):
        return pltpu.make_async_remote_copy(
            src_ref=w_v.at[i], dst_ref=w_v.at[i],
            send_sem=pass_send.at[i], recv_sem=w_sem.at[i],
            device_id={"replica": head + 3}, device_id_type=MESH)

    def bias_copies():
        return [
            pltpu.make_async_remote_copy(
                src_ref=bias_v, dst_ref=bias_v,
                send_sem=bias_send.at[step], recv_sem=bias_recv,
                device_id={"replica": head + step}, device_id_type=MESH)
            for step in range(1, GROUP)
        ]

    def prepare(blocks):
        gain_row = gain[...].astype(jnp.float32).reshape(1, depth)
        for block in blocks:
            load_hidden(block).wait()
            for i in range(block * SUB // HEAD, (block + 1) * SUB // HEAD):
                part = pl.ds(i * HEAD, HEAD)
                total = jnp.zeros((HEAD, HEAD), jnp.float32)
                for j in range(depth // HEAD):
                    cols = slice(j * HEAD, (j + 1) * HEAD)
                    piece = h_v[part, cols].astype(jnp.float32)
                    total = total + piece * piece
                    n_v[part, cols] = (piece * gain_row[:, cols]).astype(jnp.bfloat16)
                squares[0, pl.ds(i, 1), :] = jnp.sum(total.T, axis=0, keepdims=True)

    kept = rows - MOVED
    other = head + lax.rem(slot + 2, GROUP)

    def move_copy():
        return pltpu.make_async_remote_copy(
            src_ref=n_v.at[pl.ds(kept, MOVED)], dst_ref=n_v.at[pl.ds(rows, MOVED)],
            send_sem=move_sem.at[0], recv_sem=move_sem.at[1],
            device_id={"replica": other}, device_id_type=MESH)

    def back_copy():
        return pltpu.make_async_remote_copy(
            src_ref=moved_v, dst_ref=sums_v.at[pl.ds(kept, MOVED)],
            send_sem=back_sem.at[0], recv_sem=back_sem.at[1],
            device_id={"replica": other}, device_id_type=MESH)

    def send_weight(blocks):
        for i in blocks:
            if 2 < i < last and i % 2 == 1:
                mix(far - 1 - i // 2)
            if i == last:
                load_whole(last).wait()
            for copy in head_copies(i):
                copy.start()

    load_gain.wait()
    early = range(subs // 2)
    late = range(subs // 2, subs)

    @pl.when(slot == 0)
    def _():
        load_whole(0).wait()
        mix(far - 1)
        pl.semaphore_wait(barrier, waits)
        send_weight(range(ring))
        prepare(range(subs))

    @pl.when(slot == 1)
    def _():
        prepare(range(subs))
        pl.semaphore_wait(barrier, waits)

    @pl.when(slot > 1)
    def _():
        prepare(late)
        pl.semaphore_wait(barrier, waits)
        move_copy().start()
        prepare(early)

    def square_copy(distance):
        return pltpu.make_async_remote_copy(
            src_ref=squares.at[0], dst_ref=squares.at[distance],
            send_sem=square_send.at[distance], recv_sem=square_recv.at[distance],
            device_id={"tensor": at(distance)}, device_id_type=MESH)

    for distance in range(1, ring):
        square_copy(distance).start()
    load_bias.wait()

    @pl.when(slot == 0)
    def _():
        bias_v[...] = jnp.broadcast_to(bias[...], bias_v.shape)
        for copy in bias_copies():
            copy.start()

    def take_weight(i):
        @pl.when(slot > 0)
        def _():
            pass_copy(i).wait_recv()

        @pl.when(slot == 2)
        def _():
            pass_copy(i).start()

    inside_a = [(0, rows // 2), (rows // 2, rows // 2), (rows, MOVED)]
    inside_b = [(0, kept // 2), (kept // 2, kept // 2)]

    def product(i, rows_of):
        start, size = rows_of
        return jnp.dot(n_v[pl.ds(start, size), :], w_v[i], preferred_element_type=jnp.float32)

    def trade_rows(value):
        size = value.shape[0] // 2
        return trade(value[:size], value[size:])

    def hop(distance, positive):
        return (distance - 1) + (0 if positive else far)

    def starts(positive, seg, half):
        return ((seg, half) in ((0, 0), (0, 1), (2, 0))) == positive

    def ring_pass(segments):
        def ring_copy(distance, positive, half, seg):
            h = hop(distance, positive)
            start, size = segments[seg]
            part = pl.ds(start // 2, size // 2)
            return pltpu.make_async_remote_copy(
                src_ref=send_v.at[h, half, part], dst_ref=recv_v.at[h, half, part],
                send_sem=ring_send.at[h, half, seg], recv_sem=ring_recv.at[h, half, seg],
                device_id={"tensor": at(1 if positive else -1)}, device_id_type=MESH)

        def incoming(distance, positive, half, seg):
            ring_copy(distance, positive, half, seg).wait_recv()
            start, size = segments[seg]
            return recv_v[hop(distance, positive), half, pl.ds(start // 2, size // 2)].astype(jnp.float32)

        started = []

        def forward(distance, positive, half, seg, value):
            start, size = segments[seg]
            send_v[hop(distance, positive), half, pl.ds(start // 2, size // 2)] = value.astype(jnp.bfloat16)
            copy = ring_copy(distance, positive, half, seg)
            copy.start()
            started.append(copy)

        def stage(i, seg):
            value = trade_rows(product(i, segments[seg]))
            if i == 0:
                for half, packed in enumerate(value):
                    forward(far, starts(True, seg, half), half, seg, packed)
                return
            k, half = far - 1 - (i - 1) // 2, (i - 1) % 2
            ways = [(True, value[0]), (False, value[1])]
            if k == far - 1 and starts(True, seg, half):
                ways = ways[::-1]
            for positive, packed in ways:
                if k < far - 1 or starts(positive, seg, half):
                    packed = packed + incoming(k + 1, positive, half, seg)
                forward(k, positive, half, seg, packed)

        def total(seg):
            value = product(last, segments[seg])
            halves = [incoming(1, True, half, seg) + incoming(1, False, half, seg) for half in (0, 1)]
            return value + jnp.concatenate(trade(*halves), axis=0)

        def drain():
            for copy in started:
                copy.wait_send()

        return stage, total, drain

    def ready():
        load_table.wait()
        load_lens.wait()
        sums = squares[0]
        for distance in range(1, ring):
            square_copy(distance).wait_recv()
            sums = sums + squares[distance]

        @pl.when(slot > 0)
        def _():
            pltpu.make_async_remote_copy(
                src_ref=bias_v, dst_ref=bias_v,
                send_sem=bias_send.at[1], recv_sem=bias_recv,
                device_id={"replica": head}, device_id_type=MESH).wait_recv()

        return lax.rsqrt(sums / (depth * ring) + EPSILON), bias_v[0:1, :].astype(jnp.float32)

    def finish(i, value, inverse, bias_row):
        part = pl.ds(i * HEAD, HEAD)
        lane = lax.broadcasted_iota(jnp.int32, (HEAD, HEAD), 1)
        row = lax.broadcasted_iota(jnp.int32, (HEAD, HEAD), 0)
        in_first = lane < HALF
        scale = jnp.broadcast_to(inverse[i:i + 1, :], (HEAD, HEAD)).T
        value = value * scale + bias_row
        trig = t_v[part, :]
        swapped = pltpu.roll(trig, HALF, 1)
        cosine = jnp.where(in_first, trig, swapped)
        sine = jnp.where(in_first, -swapped, trig)
        rotated = value * cosine + pltpu.roll(value, HALF, 1) * sine
        masked = jnp.where(row + i * HEAD < lens[replica], rotated, 0.0)
        out[part, :] = masked.astype(jnp.bfloat16)

    moved_at = {2: [0], 3: [1, 2], 4: [3, 4], 5: [5], 6: [6]}

    @pl.when(slot < 2)
    def _():
        stage, total, drain = ring_pass(inside_a)
        for i in range(last):
            take_weight(i)
            if i == min(moved_at):
                move_copy().wait_recv()
            for j in moved_at.get(i, []):
                stage(j, 2)
            for seg in (0, 1):
                stage(i, seg)
        take_weight(last)
        moved_v[...] = total(2)
        back_copy().start()
        inverse, bias_row = ready()
        for seg in (0, 1):
            value = total(seg)
            start, size = inside_a[seg]
            for r in range(0, size, HEAD):
                finish((start + r) // HEAD, value[r:r + HEAD], inverse, bias_row)
        drain()
        back_copy().wait_send()

    @pl.when(slot > 1)
    def _():
        stage, total, drain = ring_pass(inside_b)
        for i in range(last):
            take_weight(i)
            for seg in (0, 1):
                stage(i, seg)
        take_weight(last)
        inverse, bias_row = ready()
        done = 0
        for seg, (start, size) in enumerate(inside_b):
            sums_v[pl.ds(start, size), :] = total(seg)
            for i in range(done, (start + size) // HEAD):
                finish(i, sums_v[pl.ds(i * HEAD, HEAD), :], inverse, bias_row)
            done = (start + size) // HEAD
        back_copy().wait_recv()
        for i in range(done, rows // HEAD):
            finish(i, sums_v[pl.ds(i * HEAD, HEAD), :], inverse, bias_row)
        drain()
        move_copy().wait_send()

    for distance in range(1, ring):
        square_copy(distance).wait_send()

    @pl.when(slot == 0)
    def _():
        for i in range(ring):
            for copy in head_copies(i):
                copy.wait_send()
        for copy in bias_copies():
            copy.wait_send()

    @pl.when(slot == 2)
    def _():
        for i in range(ring):
            pass_copy(i).wait_send()


def solution(mesh):
    ring = mesh.shape["tensor"]

    def local(hidden, norm_gain, layer_weight, layer_bias, lengths):
        rows, depth = hidden.shape
        subs = rows // SUB
        far = ring // 2
        table = jnp.asarray(rope_table(rows))
        dma = pltpu.SemaphoreType.DMA
        arrays = (hidden, norm_gain, layer_weight, layer_bias, lengths, table)
        return pl.pallas_call(
            functools.partial(kernel, ring),
            out_shape=jax.ShapeDtypeStruct((rows, HEAD), jnp.bfloat16),
            in_specs=[pl.BlockSpec(memory_space=pl.ANY)] * 6,
            out_specs=pl.BlockSpec(memory_space=pltpu.VMEM),
            scratch_shapes=[
                pltpu.VMEM((rows, depth), jnp.bfloat16),
                pltpu.VMEM((rows + MOVED, depth), jnp.bfloat16),
                pltpu.VMEM((ring - 2, depth, HEAD), jnp.bfloat16),
                pltpu.VMEM((ring, depth, HEAD), jnp.bfloat16),
                pltpu.VMEM((rows, HEAD), jnp.float32),
                pltpu.VMEM((depth,), jnp.bfloat16),
                pltpu.VMEM((1, HEAD), jnp.bfloat16),
                pltpu.SMEM(lengths.shape, jnp.int32),
                pltpu.VMEM((ring, rows // HEAD, HEAD), jnp.float32),
                pltpu.VMEM((16, HEAD), jnp.bfloat16),
                pltpu.VMEM((rows, HEAD), jnp.float32),
                pltpu.VMEM((MOVED, HEAD), jnp.float32),
                pltpu.VMEM((2 * far, 2, (rows + MOVED) // 2, HEAD), jnp.bfloat16),
                pltpu.VMEM((2 * far, 2, (rows + MOVED) // 2, HEAD), jnp.bfloat16),
                dma((subs,)),
                dma,
                dma((3,)),
                dma((ring - 2,)),
                dma((ring,)),
                dma((ring, 2)),
                dma((ring,)),
                dma((ring,)),
                dma((ring,)),
                dma((GROUP,)),
                dma,
                dma((2,)),
                dma((2,)),
                dma((2 * far, 2, 3)),
                dma((2 * far, 2, 3)),
            ],
            compiler_params=pltpu.CompilerParams(
                collective_id=0, has_side_effects=True, vmem_limit_bytes=48 * 1024 * 1024
            ),
            name="keys",
        )(*(pltpu.with_memory_space_constraint(x, pltpu.HBM) for x in arrays))

    in_specs = (
        P("replica", "tensor"),
        P("tensor"),
        P("replica", "tensor", None),
        P("replica", "tensor"),
        P(),
    )
    return jax.shard_map(
        local, mesh=mesh, in_specs=in_specs, out_specs=P("replica", "tensor"), check_vma=False
    )
```

```python
import functools

import jax
import jax.numpy as jnp
import numpy as np
from jax import lax
from jax.experimental import pallas as pl
from jax.experimental.pallas import tpu as pltpu
from jax.sharding import PartitionSpec as P

HEAD = 128
HALF = HEAD // 2
GROUP = 4
SUB = 512
MOVED = 64
READY_AFTER = 4
EPSILON = 1e-06
ROPE_BASE = 1000000.0
MESH = pl.DeviceIdType.MESH


def rope_table(rows):
    exponent = np.arange(HALF, dtype=np.float32) * np.float32(2.0 / HEAD)
    frequency = np.float32(1.0) / np.power(np.float32(ROPE_BASE), exponent)
    angles = np.arange(rows, dtype=np.float32)[:, None] * frequency[None, :]
    angles = angles.astype(np.float64)
    return np.concatenate([np.cos(angles), np.sin(angles)], axis=1).astype(np.float32)


def trade(x, y):
    first = lax.broadcasted_iota(jnp.int32, x.shape, 1) < HALF
    x_other, y_other = pltpu.roll(x, HALF, 1), pltpu.roll(y, HALF, 1)
    return jnp.where(first, x, y_other), jnp.where(first, x_other, y)


def kernel(
    ring,
    hid, gain_h, weight, bias_h, lens_h, table,
    out,
    h_v, n_v, w_n, w_v, t_v, gain, bias, lens, squares, bias_v, sums_v, moved_v, turn_v, send_v, recv_v,
    h_sem, t_sem, small_sem, n_sem, w_sem, head_send, pass_send,
    square_send, square_recv, bias_send, bias_recv, move_sem, back_sem, ring_send, ring_recv,
):
    rows, depth = h_v.shape
    subs = rows // SUB
    far = ring // 2
    replica = lax.axis_index("replica")
    z = lax.axis_index("tensor")
    slot = lax.rem(replica, GROUP)
    head = replica - slot

    def at(distance):
        return lax.rem(z + (distance + ring), ring)

    def columns(distance):
        return pl.ds(pl.multiple_of(at(distance) * HEAD, HEAD), HEAD)

    barrier = pltpu.get_barrier_semaphore()
    for step in range(1, GROUP):
        other = head + lax.rem(slot + step, GROUP)
        pl.semaphore_signal(barrier, inc=1, device_id={"replica": other}, device_id_type=MESH)
    for distance in range(1, ring):
        pl.semaphore_signal(barrier, inc=1, device_id={"tensor": at(distance)}, device_id_type=MESH)
    waits = ring - 1 + GROUP - 1

    def load_hidden(block):
        part = pl.ds(block * SUB, SUB)
        return pltpu.make_async_copy(hid.at[part], h_v.at[part], h_sem.at[block])

    last = ring - 1

    def load_whole(i):
        distance = far if i == 0 else 0
        return pltpu.make_async_copy(weight.at[0, :, columns(distance)], w_v.at[i], w_sem.at[i])

    def load_part(k, sign):
        j = 2 * (k - 1) + (0 if sign > 0 else 1)
        return pltpu.make_async_copy(weight.at[0, :, columns(sign * k)], w_n.at[j], n_sem.at[j])

    load_table = pltpu.make_async_copy(table, t_v, t_sem)
    load_gain = pltpu.make_async_copy(gain_h, gain, small_sem.at[0])
    load_bias = pltpu.make_async_copy(bias_h, bias, small_sem.at[1])
    load_lens = pltpu.make_async_copy(lens_h, lens, small_sem.at[2])

    @pl.when(slot == 0)
    def _():
        load_whole(0).start()
        for k in range(far - 1, 0, -1):
            load_part(k, 1).start()
            load_part(k, -1).start()
        load_whole(last).start()

    load_gain.start()
    for block in range(subs):
        load_hidden(block).start()
    load_bias.start()
    load_lens.start()
    load_table.start()

    def block_of(k, half):
        return 1 + 2 * (far - 1 - k) + half

    def mix(k):
        load_part(k, 1).wait()
        load_part(k, -1).wait()
        j = 2 * (k - 1)
        for r in range(0, depth, HEAD):
            part = pl.ds(r, HEAD)
            plus = w_n[j, part].astype(jnp.float32)
            minus = w_n[j + 1, part].astype(jnp.float32)
            for half, mixed in enumerate(trade(plus, minus)):
                w_v[block_of(k, half), part] = mixed.astype(jnp.bfloat16)

    def head_copies(i):
        return [
            pltpu.make_async_remote_copy(
                src_ref=w_v.at[i], dst_ref=w_v.at[i],
                send_sem=head_send.at[i, to - 1], recv_sem=w_sem.at[i],
                device_id={"replica": head + to}, device_id_type=MESH)
            for to in (2, 1)
        ]

    def pass_copy(i):
        return pltpu.make_async_remote_copy(
            src_ref=w_v.at[i], dst_ref=w_v.at[i],
            send_sem=pass_send.at[i], recv_sem=w_sem.at[i],
            device_id={"replica": head + 3}, device_id_type=MESH)

    def bias_copies():
        return [
            pltpu.make_async_remote_copy(
                src_ref=bias_v, dst_ref=bias_v,
                send_sem=bias_send.at[step], recv_sem=bias_recv,
                device_id={"replica": head + step}, device_id_type=MESH)
            for step in range(1, GROUP)
        ]

    def prepare(blocks):
        gain_row = gain[...].astype(jnp.float32).reshape(1, depth)
        for block in blocks:
            load_hidden(block).wait()
            for i in range(block * SUB // HEAD, (block + 1) * SUB // HEAD):
                part = pl.ds(i * HEAD, HEAD)
                total = jnp.zeros((HEAD, HEAD), jnp.float32)
                for j in range(depth // HEAD):
                    cols = slice(j * HEAD, (j + 1) * HEAD)
                    piece = h_v[part, cols].astype(jnp.float32)
                    total = total + piece * piece
                    n_v[part, cols] = (piece * gain_row[:, cols]).astype(jnp.bfloat16)
                squares[0, pl.ds(i, 1), :] = jnp.sum(total.T, axis=0, keepdims=True)

    kept = rows - MOVED
    other = head + lax.rem(slot + 2, GROUP)

    def move_copy():
        return pltpu.make_async_remote_copy(
            src_ref=n_v.at[pl.ds(kept, MOVED)], dst_ref=n_v.at[pl.ds(rows, MOVED)],
            send_sem=move_sem.at[0], recv_sem=move_sem.at[1],
            device_id={"replica": other}, device_id_type=MESH)

    def back_copy():
        return pltpu.make_async_remote_copy(
            src_ref=moved_v, dst_ref=sums_v.at[pl.ds(kept, MOVED)],
            send_sem=back_sem.at[0], recv_sem=back_sem.at[1],
            device_id={"replica": other}, device_id_type=MESH)

    def send_weight(blocks):
        for i in blocks:
            if 2 < i < last and i % 2 == 1:
                mix(far - 1 - i // 2)
            if i == last:
                load_whole(last).wait()
            for copy in head_copies(i):
                copy.start()

    load_gain.wait()
    load_bias.wait()
    early = range(subs // 2)
    late = range(subs // 2, subs)

    @pl.when(slot == 0)
    def _():
        load_whole(0).wait()
        mix(far - 1)
        bias_v[...] = jnp.broadcast_to(bias[...], bias_v.shape)
        pl.semaphore_wait(barrier, waits)
        for copy in bias_copies():
            copy.start()
        send_weight(range(ring))
        prepare(range(subs))

    @pl.when(slot == 1)
    def _():
        prepare(range(subs))
        pl.semaphore_wait(barrier, waits)

    @pl.when(slot > 1)
    def _():
        prepare(late)
        pl.semaphore_wait(barrier, waits)
        move_copy().start()
        prepare(early)

    def square_copy(distance):
        return pltpu.make_async_remote_copy(
            src_ref=squares.at[0], dst_ref=squares.at[distance],
            send_sem=square_send.at[distance], recv_sem=square_recv.at[distance],
            device_id={"tensor": at(distance)}, device_id_type=MESH)

    for distance in range(1, ring):
        square_copy(distance).start()
    def take_weight(i):
        @pl.when(slot > 0)
        def _():
            pass_copy(i).wait_recv()

        @pl.when(slot == 2)
        def _():
            pass_copy(i).start()

    inside_a = [(0, rows // 2), (rows // 2, rows // 2), (rows, MOVED)]
    inside_b = [(start, min(rows // 4, kept - start)) for start in range(0, kept, rows // 4)]

    def product(i, rows_of):
        start, size = rows_of
        return jnp.dot(n_v[pl.ds(start, size), :], w_v[i], preferred_element_type=jnp.float32)

    def trade_rows(value):
        size = value.shape[0] // 2
        return trade(value[:size], value[size:])

    def hop(distance, positive):
        return (distance - 1) + (0 if positive else far)

    def ring_pass(segments):
        def starts(positive, seg, half):
            if segments[seg][0] == rows:
                return (half == 0) == positive
            return (segments[seg][0] < rows // 2) == positive

        def ring_copy(distance, positive, half, seg):
            h = hop(distance, positive)
            start, size = segments[seg]
            part = pl.ds(start // 2, size // 2)
            return pltpu.make_async_remote_copy(
                src_ref=send_v.at[h, half, part], dst_ref=recv_v.at[h, half, part],
                send_sem=ring_send.at[h, half, seg], recv_sem=ring_recv.at[h, half, seg],
                device_id={"tensor": at(1 if positive else -1)}, device_id_type=MESH)

        def incoming(distance, positive, half, seg):
            ring_copy(distance, positive, half, seg).wait_recv()
            start, size = segments[seg]
            return recv_v[hop(distance, positive), half, pl.ds(start // 2, size // 2)].astype(jnp.float32)

        started = []

        def forward(distance, positive, half, seg, value):
            start, size = segments[seg]
            send_v[hop(distance, positive), half, pl.ds(start // 2, size // 2)] = value.astype(jnp.bfloat16)
            copy = ring_copy(distance, positive, half, seg)
            copy.start()
            started.append(copy)

        def stage(i, seg):
            value = trade_rows(product(i, segments[seg]))
            if i == 0:
                for half, packed in enumerate(value):
                    forward(far, starts(True, seg, half), half, seg, packed)
                return
            k, half = far - 1 - (i - 1) // 2, (i - 1) % 2
            ways = [(True, value[0]), (False, value[1])]
            if k == far - 1 and starts(True, seg, half):
                ways = ways[::-1]
            for positive, packed in ways:
                if k < far - 1 or starts(positive, seg, half):
                    packed = packed + incoming(k + 1, positive, half, seg)
                forward(k, positive, half, seg, packed)

        def total(seg):
            value = product(last, segments[seg])
            halves = [incoming(1, True, half, seg) + incoming(1, False, half, seg) for half in (0, 1)]
            return value + jnp.concatenate(trade(*halves), axis=0)

        def drain():
            for copy in started:
                copy.wait_send()

        return stage, total, drain

    def ready():
        load_table.wait()
        load_lens.wait()
        sums = squares[0]
        for distance in range(1, ring):
            square_copy(distance).wait_recv()
            sums = sums + squares[distance]

        @pl.when(slot > 0)
        def _():
            pltpu.make_async_remote_copy(
                src_ref=bias_v, dst_ref=bias_v,
                send_sem=bias_send.at[1], recv_sem=bias_recv,
                device_id={"replica": head}, device_id_type=MESH).wait_recv()

        inverse = lax.rsqrt(sums / (depth * ring) + EPSILON)
        bias_rows = jnp.broadcast_to(bias_v[0:1, :].astype(jnp.float32), (HEAD, HEAD))
        bias_other = pltpu.roll(bias_rows, HALF, 1)
        in_first = lax.broadcasted_iota(jnp.int32, (HEAD, HEAD), 1) < HALF
        for i in range(rows // HEAD):
            part = pl.ds(i * HEAD, HEAD)
            scale = jnp.broadcast_to(inverse[i:i + 1, :], (HEAD, HEAD)).T
            trig = t_v[part, :]
            swapped = pltpu.roll(trig, HALF, 1)
            cosine = jnp.where(in_first, trig, swapped)
            sine = jnp.where(in_first, -swapped, trig)
            turn_v[0, part, :] = scale * cosine
            turn_v[1, part, :] = scale * sine
            turn_v[2, part, :] = bias_rows * cosine + bias_other * sine

    def finish(i, value):
        part = pl.ds(i * HEAD, HEAD)
        row = lax.broadcasted_iota(jnp.int32, (HEAD, HEAD), 0)
        rotated = value * turn_v[0, part, :] + pltpu.roll(value, HALF, 1) * turn_v[1, part, :] + turn_v[2, part, :]
        masked = jnp.where(row + i * HEAD < lens[replica], rotated, 0.0)
        out[part, :] = masked.astype(jnp.bfloat16)

    moved_at = {2: [0], 3: [1, 2], 4: [3, 4], 5: [5], 6: [6]}

    @pl.when(slot < 2)
    def _():
        stage, total, drain = ring_pass(inside_a)
        for i in range(last):
            take_weight(i)
            if i == min(moved_at):
                move_copy().wait_recv()
            for j in moved_at.get(i, []):
                stage(j, 2)
            for seg in (0, 1):
                stage(i, seg)
            if i == READY_AFTER:
                ready()
        take_weight(last)
        moved_v[...] = total(2)
        back_copy().start()
        for seg in (0, 1):
            value = total(seg)
            start, size = inside_a[seg]
            for r in range(0, size, HEAD):
                finish((start + r) // HEAD, value[r:r + HEAD])
        drain()
        back_copy().wait_send()

    @pl.when(slot > 1)
    def _():
        stage, total, drain = ring_pass(inside_b)
        for i in range(last):
            take_weight(i)
            for seg in range(len(inside_b)):
                stage(i, seg)
            if i == READY_AFTER:
                ready()
        take_weight(last)
        done = 0
        for seg, (start, size) in enumerate(inside_b):
            sums_v[pl.ds(start, size), :] = total(seg)
            for i in range(done, (start + size) // HEAD):
                finish(i, sums_v[pl.ds(i * HEAD, HEAD), :])
            done = (start + size) // HEAD
        back_copy().wait_recv()
        for i in range(done, rows // HEAD):
            finish(i, sums_v[pl.ds(i * HEAD, HEAD), :])
        drain()
        move_copy().wait_send()

    for distance in range(1, ring):
        square_copy(distance).wait_send()

    @pl.when(slot == 0)
    def _():
        for i in range(ring):
            for copy in head_copies(i):
                copy.wait_send()
        for copy in bias_copies():
            copy.wait_send()

    @pl.when(slot == 2)
    def _():
        for i in range(ring):
            pass_copy(i).wait_send()


def solution(mesh):
    ring = mesh.shape["tensor"]

    def local(hidden, norm_gain, layer_weight, layer_bias, lengths):
        rows, depth = hidden.shape
        subs = rows // SUB
        far = ring // 2
        table = jnp.asarray(rope_table(rows))
        dma = pltpu.SemaphoreType.DMA
        arrays = (hidden, norm_gain, layer_weight, layer_bias, lengths, table)
        return pl.pallas_call(
            functools.partial(kernel, ring),
            out_shape=jax.ShapeDtypeStruct((rows, HEAD), jnp.bfloat16),
            in_specs=[pl.BlockSpec(memory_space=pl.ANY)] * 6,
            out_specs=pl.BlockSpec(memory_space=pltpu.VMEM),
            scratch_shapes=[
                pltpu.VMEM((rows, depth), jnp.bfloat16),
                pltpu.VMEM((rows + MOVED, depth), jnp.bfloat16),
                pltpu.VMEM((ring - 2, depth, HEAD), jnp.bfloat16),
                pltpu.VMEM((ring, depth, HEAD), jnp.bfloat16),
                pltpu.VMEM((rows, HEAD), jnp.float32),
                pltpu.VMEM((depth,), jnp.bfloat16),
                pltpu.VMEM((1, HEAD), jnp.bfloat16),
                pltpu.SMEM(lengths.shape, jnp.int32),
                pltpu.VMEM((ring, rows // HEAD, HEAD), jnp.float32),
                pltpu.VMEM((16, HEAD), jnp.bfloat16),
                pltpu.VMEM((rows, HEAD), jnp.float32),
                pltpu.VMEM((MOVED, HEAD), jnp.float32),
                pltpu.VMEM((3, rows, HEAD), jnp.float32),
                pltpu.VMEM((2 * far, 2, (rows + MOVED) // 2, HEAD), jnp.bfloat16),
                pltpu.VMEM((2 * far, 2, (rows + MOVED) // 2, HEAD), jnp.bfloat16),
                dma((subs,)),
                dma,
                dma((3,)),
                dma((ring - 2,)),
                dma((ring,)),
                dma((ring, 2)),
                dma((ring,)),
                dma((ring,)),
                dma((ring,)),
                dma((GROUP,)),
                dma,
                dma((2,)),
                dma((2,)),
                dma((2 * far, 2, 4)),
                dma((2 * far, 2, 4)),
            ],
            compiler_params=pltpu.CompilerParams(
                collective_id=0, has_side_effects=True, vmem_limit_bytes=48 * 1024 * 1024
            ),
            name="keys",
        )(*(pltpu.with_memory_space_constraint(x, pltpu.HBM) for x in arrays))

    in_specs = (
        P("replica", "tensor"),
        P("tensor"),
        P("replica", "tensor", None),
        P("replica", "tensor"),
        P(),
    )
    return jax.shard_map(
        local, mesh=mesh, in_specs=in_specs, out_specs=P("replica", "tensor"), check_vma=False
    )
```
